32 devices in a mesh: row: 8 (over y, x, core), col: 4 (over z).
Axes of the slice: x: 2, y: 2, z: 4, core: 2. Of those that a mesh axis runs over, the one named last changes fastest.
Arguments:
- trail_adjoint: float32 [4, 8, 128, 8, 4, 128], P(None, 'row', None, None, 'col'), may hold values from -24 to 24, as said below
- factor_panels: float32 [4, 8, 128, 2, 128], P(None, 'row'), may hold values from -1 to 2, as said below
- factor_adjoint: float32 [4, 8, 128, 2, 128], P(None, 'row'), may hold values from -6 to 6
- diag_inverse: float32 [2, 128, 128], replicated, may hold values from -1 to 1, as said below
Outputs:
- cov_adjoint: float32 [4, 8, 128, 8, 4, 128], P(None, 'row', None, None, 'col')
The draws below stay inside these ranges and needn't reach their ends.
Inputs may be any that keep to these rules, and one draw needn't show every extreme that they name: trail_adjoint read as the matrix H is symmetric. `factor_panels`: read as Lp, panel k is zero on rows before k * 128, and its rows D_k form a lower triangular block with diagonal entries from 1 to 2. diag_inverse[k] is the inverse of the lower triangular block of panel k on the rows D_k.
All inputs are finite; a program needn't handle non-finite values.
Results may differ from the reference program's by a relative error of at most 0.0002.
Values sent between devices are 32-bit elements; how exact they have to be, the bound alone decides.
A program may use at most 64 MiB of HBM per device.

```python
import math
import jax
import jax.numpy as jnp
from jax import lax

NB = 128
TR_DEV = 4
TC_DEV = 8
ORDER = 4096
N_ROW = 8
N_COL = 4


def factor_blocks(key):
    base_key = jax.random.fold_in(key, 11)
    blocks = []
    inverses = []
    half = NB // 2
    lower_half = (jnp.arange(NB) >= half)[:, None]
    upper_half = (jnp.arange(NB) < half)[None, :]
    coupling_mask = jnp.logical_and(lower_half, upper_half)
    identity = jnp.eye(NB, dtype=jnp.float32)
    for panel_index in range(2):
        panel_key = jax.random.fold_in(base_key, panel_index)
        diag_key, off_key = jax.random.split(panel_key)
        diagonal = jax.random.uniform(diag_key, (NB,), jnp.float32, 1.0, 2.0)
        spread = jax.random.truncated_normal(off_key, -2.0, 2.0, (NB, NB), jnp.float32) * (1.0 / math.sqrt(NB))
        coupling = jnp.where(coupling_mask, spread, 0.0)
        blocks.append(diagonal[:, None] * (identity + coupling))
        inverses.append((identity - coupling) / diagonal[None, :])
    return (blocks, inverses)


def draw_factor_panels(key, part):
    blocks, inverses = factor_blocks(key)
    assembled = jax.random.truncated_normal(jax.random.fold_in(key, 13), -4.0, 4.0, (ORDER, 2 * NB), jnp.float32) * (1.0 / math.sqrt(ORDER))
    assembled = assembled.at[0:NB, 0:NB].set(blocks[0])
    assembled = assembled.at[0:NB, NB:2 * NB].set(0.0)
    assembled = assembled.at[NB:2 * NB, NB:2 * NB].set(blocks[1])
    return assembled.reshape(TR_DEV, N_ROW, NB, 2, NB)


def draw_diag_inverse(key, part):
    blocks, inverses = factor_blocks(key)
    return jnp.stack(inverses)


def draw_trail_adjoint(key, part):
    drawn = jax.random.truncated_normal(jax.random.fold_in(key, 5), -4.0, 4.0, (ORDER, ORDER), jnp.float32)
    symmetric = (drawn + drawn.T) * (1.0 / math.sqrt(2.0))
    return symmetric.reshape(TR_DEV, N_ROW, NB, TC_DEV, N_COL, NB)


def levels(stream_key, dims, shards, smallest, largest):
    gain, own = 1.0, jax.random.fold_in(stream_key, 6)
    for axis_at, parts in shards:
        heights = jnp.exp(jax.random.uniform(jax.random.fold_in(own, axis_at), (parts,), jnp.float32, smallest / len(shards), largest / len(shards)))
        gain = gain * jnp.repeat(heights, dims[axis_at] // parts).reshape([-1 if axis == axis_at else 1 for axis in range(len(dims))])
    return gain


def scatter_about(rng, dims, scale, most, pieces=(), kind=jnp.bfloat16):
    array = scale * jax.random.normal(rng, dims, jnp.float32)
    if pieces:
        array = array * levels(rng, dims, pieces, -0.22, 0.18)
    return jnp.clip(array, -most, most).astype(kind)


def setup_inputs(seed: int = 0) -> dict:
    key_of = jax.random.split(jax.random.key(seed), 5)
    trail_adjoint = draw_trail_adjoint(jax.random.fold_in(key_of[4], 71), 0)
    factor_panels = draw_factor_panels(jax.random.fold_in(key_of[4], 71), 0)
    factor_adjoint = scatter_about(key_of[2], (TR_DEV, N_ROW, NB, 2, NB), 1.0, 6.0, ((1, 8),), jnp.float32)
    diag_inverse = draw_diag_inverse(jax.random.fold_in(key_of[4], 71), 0)
    return dict(trail_adjoint=trail_adjoint, factor_panels=factor_panels, factor_adjoint=factor_adjoint, diag_inverse=diag_inverse)


def product(left_matrix, right_matrix):
    return jnp.dot(left_matrix, right_matrix, precision=lax.Precision.HIGHEST, preferred_element_type=jnp.float32)


def halved_lower(matrix):
    return jnp.tril(matrix) - 0.5 * matrix * jnp.eye(matrix.shape[0], dtype=matrix.dtype)


def diagonal_adjoint(lower_block, given_block, gram_block, inverse):
    reduced = jnp.tril(given_block - gram_block)
    inner_block = halved_lower(product(lower_block.T, reduced))
    mixed_block = product(product(inverse.T, inner_block), inverse)
    return 0.5 * (mixed_block + mixed_block.T)


def reference(trail_adjoint, factor_panels, factor_adjoint, diag_inverse):
    matrix = trail_adjoint.reshape(ORDER, ORDER)
    lower_panels = factor_panels.reshape(ORDER, 2 * NB)
    given_panels = factor_adjoint.reshape(ORDER, 2 * NB)
    all_rows = jnp.arange(ORDER, dtype=jnp.int32)
    for panel_index in (1, 0):
        start_col = panel_index * NB
        stop_col = start_col + NB
        below_mask = (all_rows >= stop_col)[:, None]
        lower_cols = jnp.where(below_mask, lower_panels[:, start_col:stop_col], 0.0)
        products = product(matrix, lower_cols)
        adjoint_cols = jnp.where(below_mask, given_panels[:, start_col:stop_col] - 2.0 * products, 0.0)
        scaled = product(adjoint_cols, diag_inverse[panel_index])
        gram_block = product(scaled.T, lower_cols)
        diag_update = diagonal_adjoint(lower_panels[start_col:stop_col, start_col:stop_col], given_panels[start_col:stop_col, start_col:stop_col], gram_block, diag_inverse[panel_index])
        matrix = matrix.at[:, start_col:stop_col].add(0.5 * scaled)
        matrix = matrix.at[start_col:stop_col, :].add(0.5 * scaled.T)
        matrix = matrix.at[start_col:stop_col, start_col:stop_col].add(diag_update)
    return matrix.reshape(trail_adjoint.shape)
```

```python
import functools

import jax
import jax.numpy as jnp
from jax import lax
from jax.experimental import pallas as pl
from jax.experimental.pallas import tpu as pltpu
from jax.sharding import PartitionSpec as P

MESH = pl.DeviceIdType.MESH


def dot(a, b, ca=1, cb=0):
    return lax.dot_general(
        a,
        b,
        (((ca,), (cb,)), ((), ())),
        precision=lax.Precision.HIGHEST,
        preferred_element_type=jnp.float32,
    )


def halved_lower(matrix):
    rows = lax.broadcasted_iota(jnp.int32, matrix.shape, 0)
    cols = lax.broadcasted_iota(jnp.int32, matrix.shape, 1)
    return jnp.where(rows > cols, matrix, jnp.where(rows == cols, 0.5 * matrix, 0.0))


def lower(matrix):
    rows = lax.broadcasted_iota(jnp.int32, matrix.shape, 0)
    cols = lax.broadcasted_iota(jnp.int32, matrix.shape, 1)
    return jnp.where(rows >= cols, matrix, 0.0)


def diagonal_adjoint(lower_block, given_block, gram_block, inverse):
    inner = halved_lower(dot(lower_block, lower(given_block - gram_block), 0, 0))
    mixed = dot(dot(inverse, inner, 0, 0), inverse)
    return 0.5 * (mixed + mixed.T)


def kernel(
    sizes,
    h_ref,
    lp_ref,
    lb_ref,
    inv_ref,
    out_ref,
    pan,
    raw,
    raw1,
    l10,
    cb,
    pbuf,
    recv,
    gpart,
    grecv,
    gred,
    g2,
    gsum,
    g3,
    ybuf,
    rowupd,
    colupd,
    cb_send,
    cb_recv,
    l_send,
    l_recv,
    raw_sem,
    p_send,
    p_recv,
    ga_send,
    ga_recv,
    gb_send,
    gb_recv,
    gc_send,
    gc_recv,
    y_send,
    row_recv,
    col_recv,
):
    n_row, n_col, R, T, nb = sizes
    s = n_row // T
    piece = 3 * nb // T
    r = lax.axis_index("row")
    c = lax.axis_index("col")
    wk = r // s
    is_worker = lax.rem(r, s) == 0
    tile = wk * n_col + c
    dst_row = lax.rem(tile, n_row)
    dst_slot = tile // n_row

    def remote(src, dst, send, receive, row, col):
        return pltpu.make_async_remote_copy(
            src_ref=src,
            dst_ref=dst,
            send_sem=send,
            recv_sem=receive,
            device_id=(row, col),
            device_id_type=MESH,
        )

    def slot_source(i):
        g = i * n_row + r
        return lax.rem(g, n_col), (g // n_col) * s

    barrier = pltpu.get_barrier_semaphore()
    for d in range(1, n_row):
        pl.semaphore_signal(
            barrier, inc=1, device_id=(lax.rem(r + d, n_row), c), device_id_type=MESH
        )
    for k in range(2):
        for i in range(R):
            src_col, src_row = slot_source(i)

            @pl.when((c == k) & (src_col != k))
            def _():
                pl.semaphore_signal(
                    barrier, inc=1, device_id=(src_row, src_col), device_id_type=MESH
                )

        for other in range(n_col):
            if other != k:

                @pl.when((c == k) & is_worker)
                def _():
                    pl.semaphore_signal(
                        barrier, inc=1, device_id=(r, other), device_id_type=MESH
                    )

    for i in range(R):
        for k in range(2):
            keep = (i * n_row + r > k) if i == 0 else True
            at = pl.ds(i * nb * 2 + k, nb, stride=2)
            lv, bv = lp_ref[at, :], lb_ref[at, :]
            if i == 0:
                lv = jnp.where(keep, lv, 0.0)
                bv = jnp.where(keep, bv, 0.0)
            pan[i, k] = lv
            pan[i, 2 + k] = bv
    for k in range(2):

        @pl.when(r == k)
        def _():
            raw[0] = lp_ref[pl.ds(k, nb, stride=2), :]
            raw[1] = lb_ref[pl.ds(k, nb, stride=2), :]

    greetings = jnp.where(c == 0, 0, 2) + jnp.where(c == 1, 0, 2)
    pl.semaphore_wait(barrier, n_row - 1 + jnp.where(is_worker, greetings, 0))

    def cb_copy(i, row):
        return remote(pan.at[i], cb, cb_send.at[i], cb_recv, row, c)

    for i in range(R):
        src_col, src_row = slot_source(i)

        @pl.when((src_col == c) & (src_row != r))
        def _():
            cb_copy(i, src_row).start()

        @pl.when((src_col == c) & (src_row == r))
        def _():
            cb[...] = pan[i]

    def l_copy(d):
        return remote(
            pan.at[0, 0], l10, l_send.at[d], l_recv, lax.rem(r + d, n_row), c
        )

    def raw_copy():
        return remote(raw, raw1, raw_sem.at[0], raw_sem.at[1], 0, c)

    @pl.when(r == 1)
    def _():
        raw_copy().start()
        for d in range(1, n_row):
            l_copy(d).start()
        l10[...] = pan[0, 0]
        raw1[...] = raw[...]

    ct = jnp.concatenate(
        [jnp.concatenate([pan[i, k] for i in range(R)], axis=0) for k in range(2)],
        axis=1,
    ).T

    def p_copy(d, w):
        return remote(
            pbuf.at[d], recv.at[r], p_send.at[d], p_recv.at[r], w * s, c
        )

    def p_step(d):
        w = lax.rem(wk + 1 + d, T)
        block = h_ref[pl.ds(w, R * nb, stride=T), :]
        part = dot(ct, block)

        @pl.when(w * s != r)
        def _():
            pbuf[d] = part
            p_copy(d, w).start()

        @pl.when(w * s == r)
        def _():
            recv[r] = part

    for d in range(T):
        p_step(d)

    out_ref[...] = h_ref[...]

    @pl.when(is_worker)
    def _():
        acc = recv[r]
        for d in range(1, n_row):
            other = lax.rem(r + n_row - d, n_row)
            remote(
                pbuf.at[0], recv.at[other], p_send.at[0], p_recv.at[other], r, c
            ).wait_recv()
            acc = acc + recv[other]

        @pl.when(dst_row != r)
        def _():
            cb_copy(0, r).wait_recv()

        z = []
        for k in range(2):
            value = cb[2 + k].T - 2.0 * acc[k * nb : (k + 1) * nb]
            z.append(jnp.where(tile > k, value, 0.0))
        gpart[0:nb] = dot(z[1], cb[1])
        gpart[nb : 2 * nb] = dot(z[1], cb[0])
        gpart[2 * nb : 3 * nb] = dot(z[0], cb[0])

        def ga_copy(d):
            w = lax.rem(wk + d, T)
            return remote(
                gpart.at[pl.ds(pl.multiple_of(w * piece, 8), piece)],
                grecv.at[wk],
                ga_send.at[d],
                ga_recv.at[wk],
                w * s,
                c,
            )

        for d in range(1, T):
            ga_copy(d).start()

        @pl.when(r != 1)
        def _():
            l_copy(1).wait_recv()

        y1 = dot(inv_ref[1], z[1], 0, 0)
        y0 = dot(inv_ref[0], z[0] - dot(l10[...], y1, 0, 0), 0, 0)
        y0, y1 = 0.5 * y0, 0.5 * y1
        ybuf[0] = y0
        ybuf[1] = y1
        ybuf[2] = y0.T
        ybuf[3] = y1.T

        def row_copy(k):
            return remote(
                ybuf.at[k], rowupd.at[wk], y_send.at[k], row_recv.at[wk], k, c
            )

        def col_copy(k):
            return remote(
                ybuf.at[2 + k],
                colupd.at[dst_slot],
                y_send.at[2 + k],
                col_recv.at[dst_slot],
                dst_row,
                k,
            )

        for k in range(2):
            own_col = (dst_row == r) & (c == k)

            @pl.when(r != k)
            def _():
                row_copy(k).start()

            @pl.when(r == k)
            def _():
                rowupd[wk] = ybuf[k]

            @pl.when(jnp.logical_not(own_col))
            def _():
                col_copy(k).start()

            @pl.when(own_col)
            def _():
                colupd[dst_slot] = ybuf[2 + k]

        total = gpart[pl.ds(pl.multiple_of(wk * piece, 8), piece)]
        for d in range(1, T):
            other = lax.rem(wk + T - d, T)
            remote(
                gpart.at[pl.ds(0, piece)],
                grecv.at[other],
                ga_send.at[0],
                ga_recv.at[other],
                r,
                c,
            ).wait_recv()
            total = total + grecv[other]
        gred[...] = total

        def gb_copy(k, source):
            return remote(
                gred, g2.at[source], gb_send.at[k], gb_recv.at[source], r, k
            )

        for k in range(2):

            @pl.when(c != k)
            def _():
                gb_copy(k, c).start()

        @pl.when(c < 2)
        def _():
            summed = gred[...]
            for d in range(1, n_col):
                other = lax.rem(c + d, n_col)
                gb_copy(0, other).wait_recv()
                summed = summed + g2[other]
            gsum[...] = summed

            def gc_copy(k):
                return remote(
                    gsum, g3.at[wk], gc_send.at[k], gc_recv.at[wk], k, c
                )

            for k in range(2):

                @pl.when(r != k)
                def _():
                    gc_copy(k).start()

                @pl.when(r == k)
                def _():
                    g3[wk] = gsum[...]

            for k in range(2):

                @pl.when(r != k)
                def _():
                    gc_copy(k).wait_send()

        for d in range(1, T):
            ga_copy(d).wait_send()
        for k in range(2):

            @pl.when(r != k)
            def _():
                row_copy(k).wait_send()

            @pl.when(jnp.logical_not((dst_row == r) & (c == k)))
            def _():
                col_copy(k).wait_send()

            @pl.when(c != k)
            def _():
                gb_copy(k, c).wait_send()

    @pl.when(jnp.logical_not(is_worker) & (r != 1))
    def _():
        l_copy(1).wait_recv()

    @pl.when(r == 0)
    def _():
        raw_copy().wait_recv()

    @pl.when(c < 2)
    def _():
        for i in range(R):
            src_col, src_row = slot_source(i)

            @pl.when(jnp.logical_not((src_col == c) & (src_row == r)))
            def _():
                remote(
                    ybuf.at[0], colupd.at[i], y_send.at[0], col_recv.at[i], r, c
                ).wait_recv()

            at = pl.ds(i * nb * T, nb, stride=T)
            out_ref[at, :] = out_ref[at, :] + colupd[i]

    @pl.when(r < 2)
    def _():
        for t in range(T):

            @pl.when(t * s != r)
            def _():
                remote(
                    ybuf.at[0], rowupd.at[t], y_send.at[0], row_recv.at[t], r, c
                ).wait_recv()

            at = pl.ds(t, nb, stride=T)
            out_ref[at, :] = out_ref[at, :] + rowupd[t]

    @pl.when((r < 2) & (c < 2))
    def _():
        for w in range(T):

            @pl.when(w * s != r)
            def _():
                remote(
                    gsum, g3.at[w], gc_send.at[0], gc_recv.at[w], r, c
                ).wait_recv()

        gram = g3[...].reshape(3 * nb, nb)
        inv0, inv1, off = inv_ref[0], inv_ref[1], l10[...]
        g1 = dot(inv1, gram[0:nb], 0, 0)
        cross = dot(inv1, gram[nb : 2 * nb], 0, 0)
        s1 = diagonal_adjoint(raw1[0], raw1[1], g1, inv1)
        extra = cross + 2.0 * dot(s1, off)
        at = pl.ds(0, nb, stride=T)

        @pl.when((r == 1) & (c == 1))
        def _():
            out_ref[at, :] = out_ref[at, :] + s1

        @pl.when((r == 1) & (c == 0))
        def _():
            out_ref[at, :] = out_ref[at, :] - 0.5 * dot(extra, inv0)

        @pl.when((r == 0) & (c == 1))
        def _():
            out_ref[at, :] = out_ref[at, :] - 0.5 * dot(extra, inv0).T

        @pl.when((r == 0) & (c == 0))
        def _():
            inner = gram[2 * nb : 3 * nb] - dot(off, cross, 0, 0) - dot(extra, off, 0, 0)
            g0 = dot(inv0, inner, 0, 0)
            s0 = diagonal_adjoint(raw[0], raw[1], g0, inv0)
            out_ref[at, :] = out_ref[at, :] + s0

    for i in range(R):
        src_col, src_row = slot_source(i)

        @pl.when((src_col == c) & (src_row != r))
        def _():
            cb_copy(i, src_row).wait_send()

    @pl.when(r == 1)
    def _():
        raw_copy().wait_send()
        for d in range(1, n_row):
            l_copy(d).wait_send()

    for d in range(T):
        w = lax.rem(wk + 1 + d, T)

        @pl.when(w * s != r)
        def _():
            p_copy(d, w).wait_send()


def per_device(n_row, n_col, trail_adjoint, factor_panels, factor_adjoint, diag_inverse):
    R, _, nb, T, _, _ = trail_adjoint.shape
    f32 = jnp.float32
    piece = 3 * nb // T
    dma = pltpu.SemaphoreType.DMA
    vmem = pl.BlockSpec(memory_space=pltpu.VMEM)
    out = pl.pallas_call(
        functools.partial(kernel, (n_row, n_col, R, T, nb)),
        out_shape=jax.ShapeDtypeStruct((R * nb * T, nb), f32),
        in_specs=[vmem] * 4,
        out_specs=vmem,
        scratch_shapes=[
            pltpu.VMEM((R, 4, nb, nb), f32),
            pltpu.VMEM((2, nb, nb), f32),
            pltpu.VMEM((2, nb, nb), f32),
            pltpu.VMEM((nb, nb), f32),
            pltpu.VMEM((4, nb, nb), f32),
            pltpu.VMEM((T, 2 * nb, nb), f32),
            pltpu.VMEM((n_row, 2 * nb, nb), f32),
            pltpu.VMEM((3 * nb, nb), f32),
            pltpu.VMEM((T, piece, nb), f32),
            pltpu.VMEM((piece, nb), f32),
            pltpu.VMEM((n_col, piece, nb), f32),
            pltpu.VMEM((piece, nb), f32),
            pltpu.VMEM((T, piece, nb), f32),
            pltpu.VMEM((4, nb, nb), f32),
            pltpu.VMEM((T, nb, nb), f32),
            pltpu.VMEM((R, nb, nb), f32),
            dma((R,)),
            dma,
            dma((n_row,)),
            dma,
            dma((2,)),
            dma((T,)),
            dma((n_row,)),
            dma((T,)),
            dma((T,)),
            dma((2,)),
            dma((n_col,)),
            dma((2,)),
            dma((T,)),
            dma((4,)),
            dma((T,)),
            dma((R,)),
        ],
        compiler_params=pltpu.CompilerParams(
            collective_id=0, has_side_effects=True, vmem_limit_bytes=40 << 20
        ),
    )(
        trail_adjoint.reshape(R * nb * T, nb),
        factor_panels.reshape(R * nb * 2, nb),
        factor_adjoint.reshape(R * nb * 2, nb),
        diag_inverse,
    )
    return out.reshape(trail_adjoint.shape)


def solution(mesh):
    placed = (
        P(None, "row", None, None, "col", None),
        P(None, "row", None, None, None),
        P(None, "row", None, None, None),
        P(),
    )
    return jax.shard_map(
        functools.partial(per_device, mesh.shape["row"], mesh.shape["col"]),
        mesh=mesh,
        in_specs=placed,
        out_specs=P(None, "row", None, None, "col", None),
        check_vma=False,
    )
```

```python
import functools

import jax
import jax.numpy as jnp
from jax import lax
from jax.experimental import pallas as pl
from jax.experimental.pallas import tpu as pltpu
from jax.sharding import PartitionSpec as P

MESH = pl.DeviceIdType.MESH


def split(x):
    high = x.astype(jnp.bfloat16)
    low = (x - high.astype(jnp.float32)).astype(jnp.bfloat16)
    return high, low


def left_parts(a):
    high, low = split(a)
    return jnp.concatenate([high, high, low], axis=1)


def right_parts(b):
    high, low = split(b)
    return jnp.concatenate([high, low, high], axis=0)


def dot_parts(left, right):
    return jnp.dot(left, right, preferred_element_type=jnp.float32)


def dot(a, b):
    return dot_parts(left_parts(a), right_parts(b))


def halved_lower(matrix):
    rows = lax.broadcasted_iota(jnp.int32, matrix.shape, 0)
    cols = lax.broadcasted_iota(jnp.int32, matrix.shape, 1)
    return jnp.where(rows > cols, matrix, jnp.where(rows == cols, 0.5 * matrix, 0.0))


def lower(matrix):
    rows = lax.broadcasted_iota(jnp.int32, matrix.shape, 0)
    cols = lax.broadcasted_iota(jnp.int32, matrix.shape, 1)
    return jnp.where(rows >= cols, matrix, 0.0)


def inner_block(lower_block, given_block, gram_block):
    return halved_lower(dot(lower_block.T, lower(given_block - gram_block)))


def mixed_block(inner, inverse):
    mixed = dot(dot(inverse.T, inner), inverse)
    return 0.5 * (mixed + mixed.T)


def kernel(
    sizes,
    h_hbm,
    lp_hbm,
    lb_hbm,
    inv_hbm,
    out_ref,
    lp_ref,
    lb_ref,
    inv_ref,
    pre,
    pan,
    raw,
    raw1,
    l10,
    cb,
    pbuf,
    recv,
    gpart,
    grecv,
    gred,
    g2,
    gsum,
    g3,
    ybuf,
    rowupd,
    colupd,
    cb_send,
    cb_recv,
    l_send,
    l_recv,
    raw_sem,
    p_send,
    p_recv,
    ga_send,
    ga_recv,
    gb_send,
    gb_recv,
    gc_send,
    gc_recv,
    y_send,
    row_recv,
    col_recv,
    in_sem,
    pre_send,
    pre_recv,
):
    n_row, n_col, R, T, nb = sizes
    s = n_row // T
    piece = 3 * nb // T
    r = lax.axis_index("row")
    c = lax.axis_index("col")
    wk = r // s

    def wrow(t):
        return t * s + (s - 1) * (t % 2 if isinstance(t, int) else lax.rem(t, 2))

    is_worker = wrow(wk) == r
    tile = wk * n_col + c
    dst_row = lax.rem(tile, n_row)
    dst_slot = tile // n_row

    def remote(src, dst, send, receive, row, col):
        return pltpu.make_async_remote_copy(
            src_ref=src,
            dst_ref=dst,
            send_sem=send,
            recv_sem=receive,
            device_id=(row, col),
            device_id_type=MESH,
        )

    def slot_source(i):
        g = i * n_row + r
        return lax.rem(g, n_col), wrow(g // n_col)

    reads = [
        pltpu.make_async_copy(source, target, in_sem.at[i])
        for i, (source, target) in enumerate(
            [(lp_hbm, lp_ref), (lb_hbm, lb_ref), (inv_hbm, inv_ref), (h_hbm, out_ref)]
        )
    ]
    for read in reads:
        read.start()

    barrier = pltpu.get_barrier_semaphore()
    for d in range(1, n_row):
        pl.semaphore_signal(
            barrier, inc=1, device_id=(lax.rem(r + d, n_row), c), device_id_type=MESH
        )
    for k in range(2):
        for i in range(R):
            src_col, src_row = slot_source(i)

            @pl.when((c == k) & (src_col != k))
            def _():
                pl.semaphore_signal(
                    barrier, inc=1, device_id=(src_row, src_col), device_id_type=MESH
                )

        for other in range(n_col):
            if other != k:

                @pl.when((c == k) & is_worker)
                def _():
                    pl.semaphore_signal(
                        barrier, inc=1, device_id=(r, other), device_id_type=MESH
                    )

    for read in reads[:2]:
        read.wait()

    for i in range(R):
        for k in range(2):
            keep = (i * n_row + r > k) if i == 0 else True
            at = pl.ds(i * nb * 2 + k, nb, stride=2)
            lv, bv = lp_ref[at, :], lb_ref[at, :]
            if i == 0:
                lv = jnp.where(keep, lv, 0.0)
                bv = jnp.where(keep, bv, 0.0)
            pan[i, k] = lv
            pan[i, 2 + k] = bv
    for k in range(2):

        @pl.when(r == k)
        def _():
            raw[0] = lp_ref[pl.ds(k, nb, stride=2), :]
            raw[1] = lb_ref[pl.ds(k, nb, stride=2), :]

    greetings = jnp.where(c == 0, 0, 2) + jnp.where(c == 1, 0, 2)
    pl.semaphore_wait(barrier, n_row - 1 + jnp.where(is_worker, greetings, 0))

    def cb_copy(i, row):
        return remote(pan.at[i], cb, cb_send.at[i], cb_recv, row, c)

    for i in range(R):
        src_col, src_row = slot_source(i)

        @pl.when((src_col == c) & (src_row != r))
        def _():
            cb_copy(i, src_row).start()

        @pl.when((src_col == c) & (src_row == r))
        def _():
            cb[...] = pan[i]

    def l_copy(d):
        return remote(
            pan.at[0, 0], l10, l_send.at[d], l_recv, lax.rem(r + d, n_row), c
        )

    def raw_copy():
        return remote(raw, raw1, raw_sem.at[0], raw_sem.at[1], 0, c)

    @pl.when(r == 1)
    def _():
        raw_copy().start()
        for d in range(1, n_row):
            l_copy(d).start()
        l10[...] = pan[0, 0]
        raw1[...] = raw[...]

    ct = jnp.concatenate(
        [jnp.concatenate([pan[i, k] for i in range(R)], axis=0) for k in range(2)],
        axis=1,
    ).T
    ct = left_parts(ct)
    half = T // 2
    side = lax.rem(r, 2)
    partner = r + 1 - 2 * side

    def partial(t):
        return dot_parts(ct, right_parts(out_ref[pl.ds(t, R * nb, stride=T), :]))

    def pair(d):
        return lax.rem(wk // 2 + 1 + d, half)

    def pre_copy(d):
        return remote(
            pbuf.at[d],
            pre.at[pair(d)],
            pre_send.at[d],
            pre_recv.at[pair(d)],
            partner,
            c,
        )

    def p_copy(d):
        return remote(
            pbuf.at[half + d],
            recv.at[r // 2],
            p_send.at[d],
            p_recv.at[r // 2],
            wrow(2 * pair(d) + side),
            c,
        )

    for read in reads[2:]:
        read.wait()

    for d in range(half):
        pbuf[d] = partial(2 * pair(d) + 1 - side)
        pre_copy(d).start()
    for d in range(half):
        t = 2 * pair(d) + side
        part = partial(t)
        pre_copy(d).wait_recv()
        part = part + pre[pair(d)]

        @pl.when(wrow(t) != r)
        def _():
            pbuf[half + d] = part
            p_copy(d).start()

        @pl.when(wrow(t) == r)
        def _():
            recv[r // 2] = part

    @pl.when(is_worker)
    def _():
        acc = recv[r // 2]
        for d in range(1, n_row // 2):
            other = lax.rem(r // 2 + n_row // 2 - d, n_row // 2)
            remote(
                pbuf.at[0], recv.at[other], p_send.at[0], p_recv.at[other], r, c
            ).wait_recv()
            acc = acc + recv[other]

        @pl.when(dst_row != r)
        def _():
            cb_copy(0, r).wait_recv()

        z = []
        for k in range(2):
            value = cb[2 + k].T - 2.0 * acc[k * nb : (k + 1) * nb]
            z.append(jnp.where(tile > k, value, 0.0))
        gpart[0:nb] = dot(z[1], cb[1])
        gpart[nb : 2 * nb] = dot(z[1], cb[0])
        gpart[2 * nb : 3 * nb] = dot(z[0], cb[0])

        def ga_copy(d):
            w = lax.rem(wk + d, T)
            return remote(
                gpart.at[pl.ds(pl.multiple_of(w * piece, 8), piece)],
                grecv.at[wk],
                ga_send.at[d],
                ga_recv.at[wk],
                wrow(w),
                c,
            )

        for d in range(1, T):
            ga_copy(d).start()

        @pl.when(r != 1)
        def _():
            l_copy(1).wait_recv()

        y1 = dot(inv_ref[1].T, z[1])
        y0 = dot(inv_ref[0].T, z[0] - dot(l10[...].T, y1))
        y0, y1 = 0.5 * y0, 0.5 * y1
        ybuf[0] = y0
        ybuf[1] = y1
        ybuf[2] = y0.T
        ybuf[3] = y1.T

        def row_copy(k):
            return remote(
                ybuf.at[k], rowupd.at[wk], y_send.at[k], row_recv.at[wk], k, c
            )

        def col_copy(k):
            return remote(
                ybuf.at[2 + k],
                colupd.at[dst_slot],
                y_send.at[2 + k],
                col_recv.at[dst_slot],
                dst_row,
                k,
            )

        total = gpart[pl.ds(pl.multiple_of(wk * piece, 8), piece)]
        for d in range(1, T):
            other = lax.rem(wk + T - d, T)
            remote(
                gpart.at[pl.ds(0, piece)],
                grecv.at[other],
                ga_send.at[0],
                ga_recv.at[other],
                r,
                c,
            ).wait_recv()
            total = total + grecv[other]
        gred[...] = total

        def gb_copy(k, source):
            return remote(
                gred, g2.at[source], gb_send.at[k], gb_recv.at[source], r, k
            )

        for k in range(2):

            @pl.when(c != k)
            def _():
                gb_copy(k, c).start()

        @pl.when(c < 2)
        def _():
            summed = gred[...]
            for d in range(1, n_col):
                other = lax.rem(c + d, n_col)
                gb_copy(0, other).wait_recv()
                summed = summed + g2[other]
            gsum[...] = summed

            def gc_copy(k):
                return remote(
                    gsum, g3.at[wk], gc_send.at[k], gc_recv.at[wk], k, c
                )

            for k in range(2):

                @pl.when(r != k)
                def _():
                    gc_copy(k).start()

                @pl.when(r == k)
                def _():
                    g3[wk] = gsum[...]

            for k in range(2):

                @pl.when(r != k)
                def _():
                    gc_copy(k).wait_send()

        for k in range(2):
            own_col = (dst_row == r) & (c == k)

            @pl.when(r != k)
            def _():
                row_copy(k).start()

            @pl.when(r == k)
            def _():
                rowupd[wk] = ybuf[k]

            @pl.when(jnp.logical_not(own_col))
            def _():
                col_copy(k).start()

            @pl.when(own_col)
            def _():
                colupd[dst_slot] = ybuf[2 + k]

        for d in range(1, T):
            ga_copy(d).wait_send()
        for k in range(2):

            @pl.when(r != k)
            def _():
                row_copy(k).wait_send()

            @pl.when(jnp.logical_not((dst_row == r) & (c == k)))
            def _():
                col_copy(k).wait_send()

            @pl.when(c != k)
            def _():
                gb_copy(k, c).wait_send()

    @pl.when(jnp.logical_not(is_worker) & (r != 1))
    def _():
        l_copy(1).wait_recv()

    @pl.when(r == 0)
    def _():
        raw_copy().wait_recv()

    @pl.when(c < 2)
    def _():
        for i in range(R):
            src_col, src_row = slot_source(i)

            @pl.when(jnp.logical_not((src_col == c) & (src_row == r)))
            def _():
                remote(
                    ybuf.at[0], colupd.at[i], y_send.at[0], col_recv.at[i], r, c
                ).wait_recv()

            at = pl.ds(i * nb * T, nb, stride=T)
            out_ref[at, :] = out_ref[at, :] + colupd[i]

    @pl.when(r < 2)
    def _():
        for t in range(T):

            @pl.when(wrow(t) != r)
            def _():
                remote(
                    ybuf.at[0], rowupd.at[t], y_send.at[0], row_recv.at[t], r, c
                ).wait_recv()

            at = pl.ds(t, nb, stride=T)
            out_ref[at, :] = out_ref[at, :] + rowupd[t]

    @pl.when((r < 2) & (c < 2))
    def _():
        for w in range(T):

            @pl.when(wrow(w) != r)
            def _():
                remote(
                    gsum, g3.at[w], gc_send.at[0], gc_recv.at[w], r, c
                ).wait_recv()

        gram = g3[...].reshape(3 * nb, nb)
        inv0, inv1, off = inv_ref[0], inv_ref[1], l10[...]
        g1 = dot(inv1.T, gram[0:nb])
        p1 = inner_block(raw1[0], raw1[1], g1)
        cross = dot(inv1.T, gram[nb : 2 * nb])
        at = pl.ds(0, nb, stride=T)

        @pl.when((r == 1) & (c == 1))
        def _():
            out_ref[at, :] = out_ref[at, :] + mixed_block(p1, inv1)

        @pl.when(r + c == 1)
        def _():
            moved = dot(inv1, dot(off, inv0))
            base = dot(cross, inv0)
            change = 0.5 * base + 0.5 * dot(inv1.T, dot(p1 + p1.T, moved))

            @pl.when(c == 0)
            def _():
                out_ref[at, :] = out_ref[at, :] - change

            @pl.when(c == 1)
            def _():
                out_ref[at, :] = out_ref[at, :] - change.T

        @pl.when((r == 0) & (c == 0))
        def _():
            moved = dot(inv1, off)
            tied = dot(off.T, cross)
            base = dot(inv0.T, gram[2 * nb : 3 * nb] - tied - tied.T)
            g0 = base - dot(dot(moved, inv0).T, dot(p1 + p1.T, moved))
            p0 = inner_block(raw[0], raw[1], g0)
            out_ref[at, :] = out_ref[at, :] + mixed_block(p0, inv0)

    for i in range(R):
        src_col, src_row = slot_source(i)

        @pl.when((src_col == c) & (src_row != r))
        def _():
            cb_copy(i, src_row).wait_send()

    @pl.when(r == 1)
    def _():
        raw_copy().wait_send()
        for d in range(1, n_row):
            l_copy(d).wait_send()

    for d in range(half):
        pre_copy(d).wait_send()

        @pl.when(wrow(2 * pair(d) + side) != r)
        def _():
            p_copy(d).wait_send()


def per_device(n_row, n_col, trail_adjoint, factor_panels, factor_adjoint, diag_inverse):
    R, _, nb, T, _, _ = trail_adjoint.shape
    f32 = jnp.float32
    piece = 3 * nb // T
    dma = pltpu.SemaphoreType.DMA
    vmem = pl.BlockSpec(memory_space=pltpu.VMEM)
    out = pl.pallas_call(
        functools.partial(kernel, (n_row, n_col, R, T, nb)),
        out_shape=jax.ShapeDtypeStruct((R * nb * T, nb), f32),
        in_specs=[pl.BlockSpec(memory_space=pl.ANY)] * 4,
        out_specs=vmem,
        scratch_shapes=[
            pltpu.VMEM((R * nb * 2, nb), f32),
            pltpu.VMEM((R * nb * 2, nb), f32),
            pltpu.VMEM((2, nb, nb), f32),
            pltpu.VMEM((T // 2, 2 * nb, nb), f32),
            pltpu.VMEM((R, 4, nb, nb), f32),
            pltpu.VMEM((2, nb, nb), f32),
            pltpu.VMEM((2, nb, nb), f32),
            pltpu.VMEM((nb, nb), f32),
            pltpu.VMEM((4, nb, nb), f32),
            pltpu.VMEM((T, 2 * nb, nb), f32),
            pltpu.VMEM((n_row // 2, 2 * nb, nb), f32),
            pltpu.VMEM((3 * nb, nb), f32),
            pltpu.VMEM((T, piece, nb), f32),
            pltpu.VMEM((piece, nb), f32),
            pltpu.VMEM((n_col, piece, nb), f32),
            pltpu.VMEM((piece, nb), f32),
            pltpu.VMEM((T, piece, nb), f32),
            pltpu.VMEM((4, nb, nb), f32),
            pltpu.VMEM((T, nb, nb), f32),
            pltpu.VMEM((R, nb, nb), f32),
            dma((R,)),
            dma,
            dma((n_row,)),
            dma,
            dma((2,)),
            dma((T // 2,)),
            dma((n_row // 2,)),
            dma((T,)),
            dma((T,)),
            dma((2,)),
            dma((n_col,)),
            dma((2,)),
            dma((T,)),
            dma((4,)),
            dma((T,)),
            dma((R,)),
            dma((4,)),
            dma((T // 2,)),
            dma((T // 2,)),
        ],
        compiler_params=pltpu.CompilerParams(
            collective_id=0, has_side_effects=True, vmem_limit_bytes=48 << 20
        ),
    )(
        trail_adjoint.reshape(R * nb * T, nb),
        factor_panels.reshape(R * nb * 2, nb),
        factor_adjoint.reshape(R * nb * 2, nb),
        diag_inverse,
    )
    return out.reshape(trail_adjoint.shape)


def solution(mesh):
    placed = (
        P(None, "row", None, None, "col", None),
        P(None, "row", None, None, None),
        P(None, "row", None, None, None),
        P(),
    )
    return jax.shard_map(
        functools.partial(per_device, mesh.shape["row"], mesh.shape["col"]),
        mesh=mesh,
        in_specs=placed,
        out_specs=P(None, "row", None, None, "col", None),
        check_vma=False,
    )
```

```python
import functools

import jax
import jax.numpy as jnp
from jax import lax
from jax.experimental import pallas as pl
from jax.experimental.pallas import tpu as pltpu
from jax.sharding import PartitionSpec as P

MESH = pl.DeviceIdType.MESH


def split(x):
    high = x.astype(jnp.bfloat16)
    low = (x - high.astype(jnp.float32)).astype(jnp.bfloat16)
    return high, low


def left_parts(a):
    high, low = split(a)
    return jnp.concatenate([high, high, low], axis=1)


def right_parts(b):
    high, low = split(b)
    return jnp.concatenate([high, low, high], axis=0)


def dot_parts(left, right):
    return jnp.dot(left, right, preferred_element_type=jnp.float32)


def dot(a, b):
    return dot_parts(left_parts(a), right_parts(b))


def halved_lower(matrix):
    rows = lax.broadcasted_iota(jnp.int32, matrix.shape, 0)
    cols = lax.broadcasted_iota(jnp.int32, matrix.shape, 1)
    return jnp.where(rows > cols, matrix, jnp.where(rows == cols, 0.5 * matrix, 0.0))


def lower(matrix):
    rows = lax.broadcasted_iota(jnp.int32, matrix.shape, 0)
    cols = lax.broadcasted_iota(jnp.int32, matrix.shape, 1)
    return jnp.where(rows >= cols, matrix, 0.0)


def inner_block(lower_block, given_block, gram_block):
    return halved_lower(dot(lower_block.T, lower(given_block - gram_block)))


def mixed_block(inner, inverse):
    mixed = dot(dot(inverse.T, inner), inverse)
    return 0.5 * (mixed + mixed.T)


def kernel(
    sizes,
    h_hbm,
    lp_hbm,
    lb_hbm,
    inv_hbm,
    out_ref,
    lp_ref,
    lb_ref,
    inv_ref,
    pre,
    pan,
    raw,
    raw1,
    l10,
    cb,
    pbuf,
    recv,
    gpart,
    grecv,
    gred,
    g2,
    gsum,
    g3,
    ybuf,
    rowupd,
    colupd,
    cb_send,
    cb_recv,
    l_send,
    l_recv,
    raw_sem,
    p_send,
    p_recv,
    ga_send,
    ga_recv,
    gb_send,
    gb_recv,
    gc_send,
    gc_recv,
    y_send,
    row_recv,
    col_recv,
    in_sem,
    pre_send,
    pre_recv,
):
    n_row, n_col, R, T, nb = sizes
    s = n_row // T
    piece = 3 * nb // T
    r = lax.axis_index("row")
    c = lax.axis_index("col")
    wk = r // s

    def wrow(t):
        return t * s + (s - 1) * (t % 2 if isinstance(t, int) else lax.rem(t, 2))

    is_worker = wrow(wk) == r
    tile = wk * n_col + c
    dst_row = lax.rem(tile, n_row)
    dst_slot = tile // n_row

    def remote(src, dst, send, receive, row, col):
        return pltpu.make_async_remote_copy(
            src_ref=src,
            dst_ref=dst,
            send_sem=send,
            recv_sem=receive,
            device_id=(row, col),
            device_id_type=MESH,
        )

    def slot_source(i):
        g = i * n_row + r
        return lax.rem(g, n_col), wrow(g // n_col)

    reads = [
        pltpu.make_async_copy(source, target, in_sem.at[i])
        for i, (source, target) in enumerate(
            [(lp_hbm, lp_ref), (lb_hbm, lb_ref), (inv_hbm, inv_ref), (h_hbm, out_ref)]
        )
    ]
    for read in reads:
        read.start()

    barrier = pltpu.get_barrier_semaphore()
    for d in range(1, n_row):
        pl.semaphore_signal(
            barrier, inc=1, device_id=(lax.rem(r + d, n_row), c), device_id_type=MESH
        )
    for k in range(2):
        for i in range(R):
            src_col, src_row = slot_source(i)

            @pl.when((c == k) & (src_col != k))
            def _():
                pl.semaphore_signal(
                    barrier, inc=1, device_id=(src_row, src_col), device_id_type=MESH
                )

        for other in range(n_col):
            if other != k:

                @pl.when((c == k) & is_worker)
                def _():
                    pl.semaphore_signal(
                        barrier, inc=1, device_id=(r, other), device_id_type=MESH
                    )

    for read in reads[:2]:
        read.wait()

    for i in range(R):
        for k in range(2):
            keep = (i * n_row + r > k) if i == 0 else True
            at = pl.ds(i * nb * 2 + k, nb, stride=2)
            lv, bv = lp_ref[at, :], lb_ref[at, :]
            if i == 0:
                lv = jnp.where(keep, lv, 0.0)
                bv = jnp.where(keep, bv, 0.0)
            pan[i, k] = lv
            pan[i, 2 + k] = bv
    for k in range(2):

        @pl.when(r == k)
        def _():
            raw[0] = lp_ref[pl.ds(k, nb, stride=2), :]
            raw[1] = lb_ref[pl.ds(k, nb, stride=2), :]

    greetings = jnp.where(c == 0, 0, 2) + jnp.where(c == 1, 0, 2)
    pl.semaphore_wait(barrier, n_row - 1 + jnp.where(is_worker, greetings, 0))

    def cb_copy(i, row):
        return remote(pan.at[i], cb, cb_send.at[i], cb_recv, row, c)

    for i in range(R):
        src_col, src_row = slot_source(i)

        @pl.when((src_col == c) & (src_row != r))
        def _():
            cb_copy(i, src_row).start()

        @pl.when((src_col == c) & (src_row == r))
        def _():
            cb[...] = pan[i]

    def l_copy(d):
        return remote(
            pan.at[0, 0], l10, l_send.at[d], l_recv, lax.rem(r + d, n_row), c
        )

    def raw_copy():
        return remote(raw, raw1, raw_sem.at[0], raw_sem.at[1], 0, c)

    @pl.when(r == 1)
    def _():
        raw_copy().start()
        for d in range(1, n_row):
            l_copy(d).start()
        l10[...] = pan[0, 0]
        raw1[...] = raw[...]

    ct = jnp.concatenate(
        [jnp.concatenate([pan[i, k] for i in range(R)], axis=0) for k in range(2)],
        axis=1,
    ).T
    ct = left_parts(ct)
    half = T // 2
    side = lax.rem(r, 2)
    partner = r + 1 - 2 * side

    def partial(t):
        return dot_parts(ct, right_parts(out_ref[pl.ds(t, R * nb, stride=T), :]))

    def pair(d):
        return lax.rem(wk // 2 + 1 + d, half)

    def pre_copy(d):
        return remote(
            pbuf.at[d],
            pre.at[pair(d)],
            pre_send.at[d],
            pre_recv.at[pair(d)],
            partner,
            c,
        )

    def p_copy(d):
        return remote(
            pbuf.at[half + d],
            recv.at[r // 2],
            p_send.at[d],
            p_recv.at[r // 2],
            wrow(2 * pair(d) + side),
            c,
        )

    for read in reads[2:]:
        read.wait()

    for d in range(half):
        pbuf[d] = partial(2 * pair(d) + 1 - side)
        pre_copy(d).start()
    for d in range(half):
        t = 2 * pair(d) + side
        part = partial(t)
        pre_copy(d).wait_recv()
        part = part + pre[pair(d)]

        @pl.when(wrow(t) != r)
        def _():
            pbuf[half + d] = part
            p_copy(d).start()

        @pl.when(wrow(t) == r)
        def _():
            recv[r // 2] = part

    @pl.when(is_worker)
    def _():
        acc = recv[r // 2]
        for d in range(1, n_row // 2):
            other = lax.rem(r // 2 + n_row // 2 - d, n_row // 2)
            remote(
                pbuf.at[0], recv.at[other], p_send.at[0], p_recv.at[other], r, c
            ).wait_recv()
            acc = acc + recv[other]

        @pl.when(dst_row != r)
        def _():
            cb_copy(0, r).wait_recv()

        z = []
        for k in range(2):
            value = cb[2 + k].T - 2.0 * acc[k * nb : (k + 1) * nb]
            z.append(jnp.where(tile > k, value, 0.0))
        gpart[0:nb] = dot(z[1], cb[1])
        gpart[nb : 2 * nb] = dot(z[1], cb[0])
        gpart[2 * nb : 3 * nb] = dot(z[0], cb[0])

        def ga_copy(d):
            w = lax.rem(wk + d, T)
            return remote(
                gpart.at[pl.ds(pl.multiple_of(w * piece, 8), piece)],
                grecv.at[wk],
                ga_send.at[d],
                ga_recv.at[wk],
                wrow(w),
                c,
            )

        for d in range(1, T):
            ga_copy(d).start()

        @pl.when(r != 1)
        def _():
            l_copy(1).wait_recv()

        y1 = dot(inv_ref[1].T, z[1])
        y0 = dot(inv_ref[0].T, z[0] - dot(l10[...].T, y1))
        y0, y1 = 0.5 * y0, 0.5 * y1
        ybuf[0] = y0
        ybuf[1] = y1
        ybuf[2] = y0.T
        ybuf[3] = y1.T

        def row_copy(k):
            return remote(
                ybuf.at[k], rowupd.at[wk], y_send.at[k], row_recv.at[wk], k, c
            )

        def col_copy(k):
            return remote(
                ybuf.at[2 + k],
                colupd.at[dst_slot],
                y_send.at[2 + k],
                col_recv.at[dst_slot],
                dst_row,
                k,
            )

        total = gpart[pl.ds(pl.multiple_of(wk * piece, 8), piece)]
        for d in range(1, T):
            other = lax.rem(wk + T - d, T)
            remote(
                gpart.at[pl.ds(0, piece)],
                grecv.at[other],
                ga_send.at[0],
                ga_recv.at[other],
                r,
                c,
            ).wait_recv()
            total = total + grecv[other]
        gred[...] = total

        def gb_copy(k, source):
            return remote(
                gred, g2.at[source], gb_send.at[k], gb_recv.at[source], r, k
            )

        for k in range(2):

            @pl.when(c != k)
            def _():
                gb_copy(k, c).start()

        @pl.when(c < 2)
        def _():
            summed = gred[...]
            for d in range(1, n_col):
                other = lax.rem(c + d, n_col)
                gb_copy(0, other).wait_recv()
                summed = summed + g2[other]
            gsum[...] = summed

            def gc_copy(k):
                return remote(
                    gsum, g3.at[wk], gc_send.at[k], gc_recv.at[wk], k, c
                )

            for k in range(2):

                @pl.when(r != k)
                def _():
                    gc_copy(k).start()

                @pl.when(r == k)
                def _():
                    g3[wk] = gsum[...]

            for k in range(2):

                @pl.when(r != k)
                def _():
                    gc_copy(k).wait_send()

        for k in range(2):
            own_col = (dst_row == r) & (c == k)

            @pl.when(r != k)
            def _():
                row_copy(k).start()

            @pl.when(r == k)
            def _():
                rowupd[wk] = ybuf[k]

            @pl.when(jnp.logical_not(own_col))
            def _():
                col_copy(k).start()

            @pl.when(own_col)
            def _():
                colupd[dst_slot] = ybuf[2 + k]

        for d in range(1, T):
            ga_copy(d).wait_send()
        for k in range(2):

            @pl.when(r != k)
            def _():
                row_copy(k).wait_send()

            @pl.when(jnp.logical_not((dst_row == r) & (c == k)))
            def _():
                col_copy(k).wait_send()

            @pl.when(c != k)
            def _():
                gb_copy(k, c).wait_send()

    @pl.when(jnp.logical_not(is_worker) & (r != 1))
    def _():
        l_copy(1).wait_recv()

    @pl.when(r == 0)
    def _():
        raw_copy().wait_recv()

    @pl.when((r < 2) & (c < 2))
    def _():
        for w in range(T):

            @pl.when(wrow(w) != r)
            def _():
                remote(
                    gsum, g3.at[w], gc_send.at[0], gc_recv.at[w], r, c
                ).wait_recv()

        gram = g3[...].reshape(3 * nb, nb)
        inv0, inv1, off = inv_ref[0], inv_ref[1], l10[...]
        g1 = dot(inv1.T, gram[0:nb])
        p1 = inner_block(raw1[0], raw1[1], g1)
        cross = dot(inv1.T, gram[nb : 2 * nb])
        at = pl.ds(0, nb, stride=T)

        @pl.when((r == 1) & (c == 1))
        def _():
            out_ref[at, :] = out_ref[at, :] + mixed_block(p1, inv1)

        @pl.when(r + c == 1)
        def _():
            moved = dot(inv1, dot(off, inv0))
            base = dot(cross, inv0)
            change = 0.5 * base + 0.5 * dot(inv1.T, dot(p1 + p1.T, moved))

            @pl.when(c == 0)
            def _():
                out_ref[at, :] = out_ref[at, :] - change

            @pl.when(c == 1)
            def _():
                out_ref[at, :] = out_ref[at, :] - change.T

        @pl.when((r == 0) & (c == 0))
        def _():
            moved = dot(inv1, off)
            tied = dot(off.T, cross)
            base = dot(inv0.T, gram[2 * nb : 3 * nb] - tied - tied.T)
            g0 = base - dot(dot(moved, inv0).T, dot(p1 + p1.T, moved))
            p0 = inner_block(raw[0], raw[1], g0)
            out_ref[at, :] = out_ref[at, :] + mixed_block(p0, inv0)

    @pl.when(c < 2)
    def _():
        for i in range(R):
            src_col, src_row = slot_source(i)

            @pl.when(jnp.logical_not((src_col == c) & (src_row == r)))
            def _():
                remote(
                    ybuf.at[0], colupd.at[i], y_send.at[0], col_recv.at[i], r, c
                ).wait_recv()

            at = pl.ds(i * nb * T, nb, stride=T)
            out_ref[at, :] = out_ref[at, :] + colupd[i]

    @pl.when(r < 2)
    def _():
        for t in range(T):

            @pl.when(wrow(t) != r)
            def _():
                remote(
                    ybuf.at[0], rowupd.at[t], y_send.at[0], row_recv.at[t], r, c
                ).wait_recv()

            at = pl.ds(t, nb, stride=T)
            out_ref[at, :] = out_ref[at, :] + rowupd[t]

    for i in range(R):
        src_col, src_row = slot_source(i)

        @pl.when((src_col == c) & (src_row != r))
        def _():
            cb_copy(i, src_row).wait_send()

    @pl.when(r == 1)
    def _():
        raw_copy().wait_send()
        for d in range(1, n_row):
            l_copy(d).wait_send()

    for d in range(half):
        pre_copy(d).wait_send()

        @pl.when(wrow(2 * pair(d) + side) != r)
        def _():
            p_copy(d).wait_send()


def per_device(n_row, n_col, trail_adjoint, factor_panels, factor_adjoint, diag_inverse):
    R, _, nb, T, _, _ = trail_adjoint.shape
    f32 = jnp.float32
    piece = 3 * nb // T
    dma = pltpu.SemaphoreType.DMA
    vmem = pl.BlockSpec(memory_space=pltpu.VMEM)
    out = pl.pallas_call(
        functools.partial(kernel, (n_row, n_col, R, T, nb)),
        out_shape=jax.ShapeDtypeStruct((R * nb * T, nb), f32),
        in_specs=[pl.BlockSpec(memory_space=pltpu.HBM)] * 4,
        out_specs=vmem,
        scratch_shapes=[
            pltpu.VMEM((R * nb * 2, nb), f32),
            pltpu.VMEM((R * nb * 2, nb), f32),
            pltpu.VMEM((2, nb, nb), f32),
            pltpu.VMEM((T // 2, 2 * nb, nb), f32),
            pltpu.VMEM((R, 4, nb, nb), f32),
            pltpu.VMEM((2, nb, nb), f32),
            pltpu.VMEM((2, nb, nb), f32),
            pltpu.VMEM((nb, nb), f32),
            pltpu.VMEM((4, nb, nb), f32),
            pltpu.VMEM((T, 2 * nb, nb), f32),
            pltpu.VMEM((n_row // 2, 2 * nb, nb), f32),
            pltpu.VMEM((3 * nb, nb), f32),
            pltpu.VMEM((T, piece, nb), f32),
            pltpu.VMEM((piece, nb), f32),
            pltpu.VMEM((n_col, piece, nb), f32),
            pltpu.VMEM((piece, nb), f32),
            pltpu.VMEM((T, piece, nb), f32),
            pltpu.VMEM((4, nb, nb), f32),
            pltpu.VMEM((T, nb, nb), f32),
            pltpu.VMEM((R, nb, nb), f32),
            dma((R,)),
            dma,
            dma((n_row,)),
            dma,
            dma((2,)),
            dma((T // 2,)),
            dma((n_row // 2,)),
            dma((T,)),
            dma((T,)),
            dma((2,)),
            dma((n_col,)),
            dma((2,)),
            dma((T,)),
            dma((4,)),
            dma((T,)),
            dma((R,)),
            dma((4,)),
            dma((T // 2,)),
            dma((T // 2,)),
        ],
        compiler_params=pltpu.CompilerParams(
            collective_id=0, has_side_effects=True, vmem_limit_bytes=48 << 20
        ),
    )(
        trail_adjoint.reshape(R * nb * T, nb),
        factor_panels.reshape(R * nb * 2, nb),
        factor_adjoint.reshape(R * nb * 2, nb),
        diag_inverse,
    )
    return out.reshape(trail_adjoint.shape)


def solution(mesh):
    placed = (
        P(None, "row", None, None, "col", None),
        P(None, "row", None, None, None),
        P(None, "row", None, None, None),
        P(),
    )
    return jax.shard_map(
        functools.partial(per_device, mesh.shape["row"], mesh.shape["col"]),
        mesh=mesh,
        in_specs=placed,
        out_specs=P(None, "row", None, None, "col", None),
        check_vma=False,
    )
```

```python
import functools

import jax
import jax.numpy as jnp
from jax import lax
from jax.experimental import pallas as pl
from jax.experimental.pallas import tpu as pltpu
from jax.sharding import PartitionSpec as P

MESH = pl.DeviceIdType.MESH


def split(x):
    high = x.astype(jnp.bfloat16)
    low = (x - high.astype(jnp.float32)).astype(jnp.bfloat16)
    return high, low


def left_parts(a):
    high, low = split(a)
    return jnp.concatenate([high, high, low], axis=1)


def right_parts(b):
    high, low = split(b)
    return jnp.concatenate([high, low, high], axis=0)


def dot_parts(left, right):
    return jnp.dot(left, right, preferred_element_type=jnp.float32)


def dot(a, b):
    return dot_parts(left_parts(a), right_parts(b))


def halved_lower(matrix):
    rows = lax.broadcasted_iota(jnp.int32, matrix.shape, 0)
    cols = lax.broadcasted_iota(jnp.int32, matrix.shape, 1)
    return jnp.where(rows > cols, matrix, jnp.where(rows == cols, 0.5 * matrix, 0.0))


def lower(matrix):
    rows = lax.broadcasted_iota(jnp.int32, matrix.shape, 0)
    cols = lax.broadcasted_iota(jnp.int32, matrix.shape, 1)
    return jnp.where(rows >= cols, matrix, 0.0)


def inner_block(lower_block, given_block, gram_block):
    return halved_lower(dot(lower_block.T, lower(given_block - gram_block)))


def mixed_block(inner, inverse):
    mixed = dot(dot(inverse.T, inner), inverse)
    return 0.5 * (mixed + mixed.T)


def kernel(
    sizes,
    h_hbm,
    lp_hbm,
    lb_hbm,
    inv_hbm,
    out_ref,
    lp_ref,
    lb_ref,
    inv_ref,
    pre,
    pan,
    raw,
    raw1,
    l10,
    cb,
    pbuf,
    recv,
    gpart,
    grecv,
    gred,
    g2,
    gsum,
    g3,
    ybuf,
    rowupd,
    colupd,
    cb_send,
    cb_recv,
    l_send,
    l_recv,
    raw_sem,
    p_send,
    p_recv,
    ga_send,
    ga_recv,
    gb_send,
    gb_recv,
    gc_send,
    gc_recv,
    y_send,
    row_recv,
    col_recv,
    in_sem,
    pre_send,
    pre_recv,
):
    n_row, n_col, R, T, nb = sizes
    s = n_row // T
    piece = 3 * nb // T
    r = lax.axis_index("row")
    c = lax.axis_index("col")
    wk = r // s

    def wrow(t):
        return t * s + (s - 1) * (t % 2 if isinstance(t, int) else lax.rem(t, 2))

    is_worker = wrow(wk) == r
    tile = wk * n_col + c
    dst_row = lax.rem(tile, n_row)
    dst_slot = tile // n_row

    def remote(src, dst, send, receive, row, col):
        return pltpu.make_async_remote_copy(
            src_ref=src,
            dst_ref=dst,
            send_sem=send,
            recv_sem=receive,
            device_id=(row, col),
            device_id_type=MESH,
        )

    def slot_source(i):
        g = i * n_row + r
        return lax.rem(g, n_col), wrow(g // n_col)

    reads = [
        pltpu.make_async_copy(source, target, in_sem.at[i])
        for i, (source, target) in enumerate(
            [(lp_hbm, lp_ref), (lb_hbm, lb_ref), (inv_hbm, inv_ref), (h_hbm, out_ref)]
        )
    ]
    for read in reads:
        read.start()

    barrier = pltpu.get_barrier_semaphore()
    for d in range(1, n_row):
        pl.semaphore_signal(
            barrier, inc=1, device_id=(lax.rem(r + d, n_row), c), device_id_type=MESH
        )
    for k in range(2):
        for i in range(R):
            src_col, src_row = slot_source(i)

            @pl.when((c == k) & (src_col != k))
            def _():
                pl.semaphore_signal(
                    barrier, inc=1, device_id=(src_row, src_col), device_id_type=MESH
                )

        for other in range(n_col):
            if other != k:

                @pl.when((c == k) & is_worker)
                def _():
                    pl.semaphore_signal(
                        barrier, inc=1, device_id=(r, other), device_id_type=MESH
                    )

    for read in reads[:2]:
        read.wait()

    for i in range(R):
        for k in range(2):
            keep = (i * n_row + r > k) if i == 0 else True
            at = pl.ds(i * nb * 2 + k, nb, stride=2)
            lv, bv = lp_ref[at, :], lb_ref[at, :]
            if i == 0:
                lv = jnp.where(keep, lv, 0.0)
                bv = jnp.where(keep, bv, 0.0)
            pan[i, k] = lv
            pan[i, 2 + k] = bv
    for k in range(2):

        @pl.when(r == k)
        def _():
            raw[0] = lp_ref[pl.ds(k, nb, stride=2), :]
            raw[1] = lb_ref[pl.ds(k, nb, stride=2), :]

    greetings = jnp.where(c == 0, 0, 2) + jnp.where(c == 1, 0, 2)
    pl.semaphore_wait(barrier, n_row - 1 + jnp.where(is_worker, greetings, 0))

    def cb_copy(i, row):
        return remote(pan.at[i, pl.ds(0, 2)], cb, cb_send.at[i], cb_recv, row, c)

    for i in range(R):
        src_col, src_row = slot_source(i)

        @pl.when((src_col == c) & (src_row != r))
        def _():
            cb_copy(i, src_row).start()

        @pl.when((src_col == c) & (src_row == r))
        def _():
            cb[0] = pan[i, 0]
            cb[1] = pan[i, 1]

    def l_copy(d):
        return remote(
            pan.at[0, 0], l10, l_send.at[d], l_recv, lax.rem(r + d, n_row), c
        )

    def raw_copy():
        return remote(raw, raw1, raw_sem.at[0], raw_sem.at[1], 0, c)

    ct = jnp.concatenate(
        [jnp.concatenate([pan[i, k] for i in range(R)], axis=0) for k in range(2)],
        axis=1,
    ).T
    ct = left_parts(ct)
    half = T // 2
    side = lax.rem(r, 2)
    partner = r + 1 - 2 * side

    def partial(t):
        return dot_parts(ct, right_parts(out_ref[pl.ds(t, R * nb, stride=T), :]))

    def pair(d):
        return lax.rem(wk // 2 + 1 + d, half)

    def pre_copy(d):
        return remote(
            pbuf.at[d],
            pre.at[pair(d)],
            pre_send.at[d],
            pre_recv.at[pair(d)],
            partner,
            c,
        )

    def p_copy(d):
        return remote(
            pbuf.at[half + d],
            recv.at[r // 2],
            p_send.at[d],
            p_recv.at[r // 2],
            wrow(2 * pair(d) + side),
            c,
        )

    for read in reads[2:]:
        read.wait()

    def fill(at, t):
        pbuf[at] = partial(t)
        g = t * n_col + c

        @pl.when(lax.rem(g, n_row) == r)
        def _():
            given = jnp.concatenate([pan[g // n_row, 2 + k].T for k in range(2)], axis=0)
            pbuf[at] = pbuf[at] - 0.5 * given

    for d in range(half):
        fill(d, 2 * pair(d) + 1 - side)
        pre_copy(d).start()
    for d in range(half):
        t = 2 * pair(d) + side
        fill(half + d, t)
        pre_copy(d).wait_recv()
        pbuf[half + d] = pbuf[half + d] + pre[pair(d)]

        @pl.when(wrow(t) != r)
        def _():
            p_copy(d).start()

        @pl.when(wrow(t) == r)
        def _():
            recv[r // 2] = pbuf[half + d]

    @pl.when(r == 1)
    def _():
        raw_copy().start()
        for d in range(1, n_row):
            l_copy(d).start()
        l10[...] = pan[0, 0]
        raw1[...] = raw[...]

    @pl.when(is_worker)
    def _():
        acc = recv[r // 2]
        for d in range(1, n_row // 2):
            other = lax.rem(r // 2 + n_row // 2 - d, n_row // 2)
            remote(
                pbuf.at[0], recv.at[other], p_send.at[0], p_recv.at[other], r, c
            ).wait_recv()
            acc = acc + recv[other]

        @pl.when(dst_row != r)
        def _():
            cb_copy(0, r).wait_recv()

        z = []
        for k in range(2):
            value = -2.0 * acc[k * nb : (k + 1) * nb]
            z.append(jnp.where(tile > k, value, 0.0))
        gpart[0:nb] = dot(z[1], cb[1])
        gpart[nb : 2 * nb] = dot(z[1], cb[0])
        gpart[2 * nb : 3 * nb] = dot(z[0], cb[0])

        def ga_copy(d):
            w = lax.rem(wk + d, T)
            return remote(
                gpart.at[pl.ds(pl.multiple_of(w * piece, 8), piece)],
                grecv.at[wk],
                ga_send.at[d],
                ga_recv.at[wk],
                wrow(w),
                c,
            )

        for d in range(1, T):
            ga_copy(d).start()

        @pl.when(r != 1)
        def _():
            l_copy(1).wait_recv()

        y1 = dot(inv_ref[1].T, z[1])
        y0 = dot(inv_ref[0].T, z[0] - dot(l10[...].T, y1))
        y0, y1 = 0.5 * y0, 0.5 * y1
        ybuf[0] = y0
        ybuf[1] = y1
        ybuf[2] = y0.T
        ybuf[3] = y1.T

        def row_copy(k):
            return remote(
                ybuf.at[k], rowupd.at[wk], y_send.at[k], row_recv.at[wk], k, c
            )

        def col_copy(k):
            return remote(
                ybuf.at[2 + k],
                colupd.at[dst_slot],
                y_send.at[2 + k],
                col_recv.at[dst_slot],
                dst_row,
                k,
            )

        total = gpart[pl.ds(pl.multiple_of(wk * piece, 8), piece)]
        for d in range(1, T):
            other = lax.rem(wk + T - d, T)
            remote(
                gpart.at[pl.ds(0, piece)],
                grecv.at[other],
                ga_send.at[0],
                ga_recv.at[other],
                r,
                c,
            ).wait_recv()
            total = total + grecv[other]
        gred[...] = total

        def gb_copy(k, source):
            return remote(
                gred, g2.at[source], gb_send.at[k], gb_recv.at[source], r, k
            )

        for k in range(2):

            @pl.when(c != k)
            def _():
                gb_copy(k, c).start()

        @pl.when(c < 2)
        def _():
            summed = gred[...]
            for d in range(1, n_col):
                other = lax.rem(c + d, n_col)
                gb_copy(0, other).wait_recv()
                summed = summed + g2[other]
            gsum[...] = summed

            def gc_copy(k):
                return remote(
                    gsum, g3.at[wk], gc_send.at[k], gc_recv.at[wk], k, c
                )

            for k in range(2):

                @pl.when(r != k)
                def _():
                    gc_copy(k).start()

                @pl.when(r == k)
                def _():
                    g3[wk] = gsum[...]

            for k in range(2):

                @pl.when(r != k)
                def _():
                    gc_copy(k).wait_send()

        for k in range(2):
            own_col = (dst_row == r) & (c == k)

            @pl.when(r != k)
            def _():
                row_copy(k).start()

            @pl.when(r == k)
            def _():
                rowupd[wk] = ybuf[k]

            @pl.when(jnp.logical_not(own_col))
            def _():
                col_copy(k).start()

            @pl.when(own_col)
            def _():
                colupd[dst_slot] = ybuf[2 + k]

        for d in range(1, T):
            ga_copy(d).wait_send()
        for k in range(2):

            @pl.when(r != k)
            def _():
                row_copy(k).wait_send()

            @pl.when(jnp.logical_not((dst_row == r) & (c == k)))
            def _():
                col_copy(k).wait_send()

            @pl.when(c != k)
            def _():
                gb_copy(k, c).wait_send()

    @pl.when(jnp.logical_not(is_worker) & (r != 1))
    def _():
        l_copy(1).wait_recv()

    @pl.when(r == 0)
    def _():
        raw_copy().wait_recv()

    @pl.when((r < 2) & (c < 2))
    def _():
        for w in range(T):

            @pl.when(wrow(w) != r)
            def _():
                remote(
                    gsum, g3.at[w], gc_send.at[0], gc_recv.at[w], r, c
                ).wait_recv()

        gram = g3[...].reshape(3 * nb, nb)
        inv0, inv1, off = inv_ref[0], inv_ref[1], l10[...]
        g1 = dot(inv1.T, gram[0:nb])
        p1 = inner_block(raw1[0], raw1[1], g1)
        cross = dot(inv1.T, gram[nb : 2 * nb])
        at = pl.ds(0, nb, stride=T)

        @pl.when((r == 1) & (c == 1))
        def _():
            out_ref[at, :] = out_ref[at, :] + mixed_block(p1, inv1)

        @pl.when(r + c == 1)
        def _():
            moved = dot(inv1, dot(off, inv0))
            base = dot(cross, inv0)
            change = 0.5 * base + 0.5 * dot(inv1.T, dot(p1 + p1.T, moved))

            @pl.when(c == 0)
            def _():
                out_ref[at, :] = out_ref[at, :] - change

            @pl.when(c == 1)
            def _():
                out_ref[at, :] = out_ref[at, :] - change.T

        @pl.when((r == 0) & (c == 0))
        def _():
            moved = dot(inv1, off)
            tied = dot(off.T, cross)
            base = dot(inv0.T, gram[2 * nb : 3 * nb] - tied - tied.T)
            g0 = base - dot(dot(moved, inv0).T, dot(p1 + p1.T, moved))
            p0 = inner_block(raw[0], raw[1], g0)
            out_ref[at, :] = out_ref[at, :] + mixed_block(p0, inv0)

    @pl.when(c < 2)
    def _():
        for i in range(R):
            src_col, src_row = slot_source(i)

            @pl.when(jnp.logical_not((src_col == c) & (src_row == r)))
            def _():
                remote(
                    ybuf.at[0], colupd.at[i], y_send.at[0], col_recv.at[i], r, c
                ).wait_recv()

            at = pl.ds(i * nb * T, nb, stride=T)
            out_ref[at, :] = out_ref[at, :] + colupd[i]

    @pl.when(r < 2)
    def _():
        for t in range(T):

            @pl.when(wrow(t) != r)
            def _():
                remote(
                    ybuf.at[0], rowupd.at[t], y_send.at[0], row_recv.at[t], r, c
                ).wait_recv()

            at = pl.ds(t, nb, stride=T)
            out_ref[at, :] = out_ref[at, :] + rowupd[t]

    for i in range(R):
        src_col, src_row = slot_source(i)

        @pl.when((src_col == c) & (src_row != r))
        def _():
            cb_copy(i, src_row).wait_send()

    @pl.when(r == 1)
    def _():
        raw_copy().wait_send()
        for d in range(1, n_row):
            l_copy(d).wait_send()

    for d in range(half):
        pre_copy(d).wait_send()

        @pl.when(wrow(2 * pair(d) + side) != r)
        def _():
            p_copy(d).wait_send()


def per_device(n_row, n_col, trail_adjoint, factor_panels, factor_adjoint, diag_inverse):
    R, _, nb, T, _, _ = trail_adjoint.shape
    f32 = jnp.float32
    piece = 3 * nb // T
    dma = pltpu.SemaphoreType.DMA
    vmem = pl.BlockSpec(memory_space=pltpu.VMEM)
    out = pl.pallas_call(
        functools.partial(kernel, (n_row, n_col, R, T, nb)),
        out_shape=jax.ShapeDtypeStruct((R * nb * T, nb), f32),
        in_specs=[pl.BlockSpec(memory_space=pltpu.HBM)] * 4,
        out_specs=vmem,
        scratch_shapes=[
            pltpu.VMEM((R * nb * 2, nb), f32),
            pltpu.VMEM((R * nb * 2, nb), f32),
            pltpu.VMEM((2, nb, nb), f32),
            pltpu.VMEM((T // 2, 2 * nb, nb), f32),
            pltpu.VMEM((R, 4, nb, nb), f32),
            pltpu.VMEM((2, nb, nb), f32),
            pltpu.VMEM((2, nb, nb), f32),
            pltpu.VMEM((nb, nb), f32),
            pltpu.VMEM((2, nb, nb), f32),
            pltpu.VMEM((T, 2 * nb, nb), f32),
            pltpu.VMEM((n_row // 2, 2 * nb, nb), f32),
            pltpu.VMEM((3 * nb, nb), f32),
            pltpu.VMEM((T, piece, nb), f32),
            pltpu.VMEM((piece, nb), f32),
            pltpu.VMEM((n_col, piece, nb), f32),
            pltpu.VMEM((piece, nb), f32),
            pltpu.VMEM((T, piece, nb), f32),
            pltpu.VMEM((4, nb, nb), f32),
            pltpu.VMEM((T, nb, nb), f32),
            pltpu.VMEM((R, nb, nb), f32),
            dma((R,)),
            dma,
            dma((n_row,)),
            dma,
            dma((2,)),
            dma((T // 2,)),
            dma((n_row // 2,)),
            dma((T,)),
            dma((T,)),
            dma((2,)),
            dma((n_col,)),
            dma((2,)),
            dma((T,)),
            dma((4,)),
            dma((T,)),
            dma((R,)),
            dma((4,)),
            dma((T // 2,)),
            dma((T // 2,)),
        ],
        compiler_params=pltpu.CompilerParams(
            collective_id=0, has_side_effects=True, vmem_limit_bytes=58 << 20
        ),
    )(
        trail_adjoint.reshape(R * nb * T, nb),
        factor_panels.reshape(R * nb * 2, nb),
        factor_adjoint.reshape(R * nb * 2, nb),
        diag_inverse,
    )
    return out.reshape(trail_adjoint.shape)


def solution(mesh):
    placed = (
        P(None, "row", None, None, "col", None),
        P(None, "row", None, None, None),
        P(None, "row", None, None, None),
        P(),
    )
    return jax.shard_map(
        functools.partial(per_device, mesh.shape["row"], mesh.shape["col"]),
        mesh=mesh,
        in_specs=placed,
        out_specs=P(None, "row", None, None, "col", None),
        check_vma=False,
    )
```

```python
import functools

import jax
import jax.numpy as jnp
from jax import lax
from jax.experimental import pallas as pl
from jax.experimental.pallas import tpu as pltpu
from jax.sharding import PartitionSpec as P

MESH = pl.DeviceIdType.MESH


def split(x):
    high = x.astype(jnp.bfloat16)
    low = (x - high.astype(jnp.float32)).astype(jnp.bfloat16)
    return high, low


def left_parts(a):
    high, low = split(a)
    return jnp.concatenate([high, high, low], axis=1)


def right_parts(b):
    high, low = split(b)
    return jnp.concatenate([high, low, high], axis=0)


def dot_parts(left, right):
    return jnp.dot(left, right, preferred_element_type=jnp.float32)


def dot(a, b):
    return dot_parts(left_parts(a), right_parts(b))


def halved_lower(matrix):
    rows = lax.broadcasted_iota(jnp.int32, matrix.shape, 0)
    cols = lax.broadcasted_iota(jnp.int32, matrix.shape, 1)
    return jnp.where(rows > cols, matrix, jnp.where(rows == cols, 0.5 * matrix, 0.0))


def lower(matrix):
    rows = lax.broadcasted_iota(jnp.int32, matrix.shape, 0)
    cols = lax.broadcasted_iota(jnp.int32, matrix.shape, 1)
    return jnp.where(rows >= cols, matrix, 0.0)


def inner_block(lower_block, given_block, gram_block):
    return halved_lower(dot(lower_block.T, lower(given_block - gram_block)))


def mixed_block(inner, inverse):
    mixed = dot(dot(inverse.T, inner), inverse)
    return 0.5 * (mixed + mixed.T)


def kernel(
    sizes,
    h_hbm,
    lp_hbm,
    lb_hbm,
    inv_hbm,
    out_ref,
    lp_ref,
    lb_ref,
    inv_ref,
    pre,
    pan,
    raw,
    raw1,
    l10,
    cb,
    pbuf,
    recv,
    gpart,
    grecv,
    gred,
    g2,
    gsum,
    g3,
    ybuf,
    rowupd,
    colupd,
    cb_send,
    cb_recv,
    l_send,
    l_recv,
    raw_sem,
    p_send,
    p_recv,
    ga_send,
    ga_recv,
    gb_send,
    gb_recv,
    gc_send,
    gc_recv,
    y_send,
    row_recv,
    col_recv,
    in_sem,
    pre_send,
    pre_recv,
):
    n_row, n_col, R, T, nb = sizes
    s = n_row // T
    piece = 3 * nb // T
    r = lax.axis_index("row")
    c = lax.axis_index("col")
    wk = r // s

    def wrow(t):
        return t * s + (s - 1) * (t % 2 if isinstance(t, int) else lax.rem(t, 2))

    is_worker = wrow(wk) == r
    tile = wk * n_col + c
    dst_row = lax.rem(tile, n_row)
    dst_slot = tile // n_row

    def remote(src, dst, send, receive, row, col):
        return pltpu.make_async_remote_copy(
            src_ref=src,
            dst_ref=dst,
            send_sem=send,
            recv_sem=receive,
            device_id=(row, col),
            device_id_type=MESH,
        )

    def slot_source(i):
        g = i * n_row + r
        return lax.rem(g, n_col), wrow(g // n_col)

    reads = [
        pltpu.make_async_copy(source, target, in_sem.at[i])
        for i, (source, target) in enumerate(
            [(lp_hbm, lp_ref), (lb_hbm, lb_ref), (inv_hbm, inv_ref), (h_hbm, out_ref)]
        )
    ]
    for read in reads:
        read.start()

    barrier = pltpu.get_barrier_semaphore()
    for d in range(1, n_row):
        pl.semaphore_signal(
            barrier, inc=1, device_id=(lax.rem(r + d, n_row), c), device_id_type=MESH
        )
    for k in range(2):
        for i in range(R):
            src_col, src_row = slot_source(i)

            @pl.when((c == k) & (src_col != k))
            def _():
                pl.semaphore_signal(
                    barrier, inc=1, device_id=(src_row, src_col), device_id_type=MESH
                )

        for other in range(n_col):
            if other != k:

                @pl.when((c == k) & is_worker)
                def _():
                    pl.semaphore_signal(
                        barrier, inc=1, device_id=(r, other), device_id_type=MESH
                    )

    for read in reads[:2]:
        read.wait()

    for i in range(R):
        for k in range(2):
            keep = (i * n_row + r > k) if i == 0 else True
            at = pl.ds(i * nb * 2 + k, nb, stride=2)
            lv, bv = lp_ref[at, :], lb_ref[at, :]
            if i == 0:
                lv = jnp.where(keep, lv, 0.0)
                bv = jnp.where(keep, bv, 0.0)
            pan[i, k] = lv
            pan[i, 2 + k] = bv
    for k in range(2):

        @pl.when(r == k)
        def _():
            raw[0] = lp_ref[pl.ds(k, nb, stride=2), :]
            raw[1] = lb_ref[pl.ds(k, nb, stride=2), :]

    greetings = jnp.where(c == 0, 0, 2) + jnp.where(c == 1, 0, 2)
    pl.semaphore_wait(barrier, n_row - 1 + jnp.where(is_worker, greetings, 0))

    def cb_copy(i, row):
        return remote(pan.at[i, pl.ds(0, 2)], cb, cb_send.at[i], cb_recv, row, c)

    for i in range(R):
        src_col, src_row = slot_source(i)

        @pl.when((src_col == c) & (src_row != r))
        def _():
            cb_copy(i, src_row).start()

        @pl.when((src_col == c) & (src_row == r))
        def _():
            cb[0] = pan[i, 0]
            cb[1] = pan[i, 1]

    def l_copy(d):
        return remote(
            pan.at[0, 0], l10, l_send.at[d], l_recv, lax.rem(r + d, n_row), c
        )

    def raw_copy():
        return remote(raw, raw1, raw_sem.at[0], raw_sem.at[1], 0, c)

    ct = jnp.concatenate(
        [jnp.concatenate([pan[i, k] for i in range(R)], axis=0) for k in range(2)],
        axis=1,
    ).T
    ct = left_parts(ct)
    half = T // 2
    side = lax.rem(r, 2)
    partner = r + 1 - 2 * side

    def partial(t):
        return dot_parts(ct, right_parts(out_ref[pl.ds(t, R * nb, stride=T), :]))

    def pair(d):
        return lax.rem(wk // 2 + 1 + d, half)

    def pre_copy(d):
        return remote(
            pbuf.at[d],
            pre.at[pair(d)],
            pre_send.at[d],
            pre_recv.at[pair(d)],
            partner,
            c,
        )

    def p_copy(d):
        return remote(
            pbuf.at[half + d],
            recv.at[r // 2],
            p_send.at[d],
            p_recv.at[r // 2],
            wrow(2 * pair(d) + side),
            c,
        )

    for read in reads[2:]:
        read.wait()

    def fill(at, t):
        pbuf[at] = partial(t)
        g = t * n_col + c

        @pl.when(lax.rem(g, n_row) == r)
        def _():
            given = jnp.concatenate([pan[g // n_row, 2 + k].T for k in range(2)], axis=0)
            pbuf[at] = pbuf[at] - 0.5 * given

    for d in range(half):
        fill(d, 2 * pair(d) + 1 - side)
        pre_copy(d).start()
    for d in range(half):
        t = 2 * pair(d) + side
        fill(half + d, t)
        pre_copy(d).wait_recv()
        pbuf[half + d] = pbuf[half + d] + pre[pair(d)]

        @pl.when(wrow(t) != r)
        def _():
            p_copy(d).start()

        @pl.when(wrow(t) == r)
        def _():
            recv[r // 2] = pbuf[half + d]

    @pl.when(r == 1)
    def _():
        raw_copy().start()
        for d in range(1, n_row):
            l_copy(d).start()
        l10[...] = pan[0, 0]
        raw1[...] = raw[...]

    @pl.when(is_worker)
    def _():
        acc = recv[r // 2]
        for d in range(1, n_row // 2):
            other = lax.rem(r // 2 + n_row // 2 - d, n_row // 2)
            remote(
                pbuf.at[0], recv.at[other], p_send.at[0], p_recv.at[other], r, c
            ).wait_recv()
            acc = acc + recv[other]

        @pl.when(dst_row != r)
        def _():
            cb_copy(0, r).wait_recv()

        z = []
        for k in range(2):
            value = -2.0 * acc[k * nb : (k + 1) * nb]
            z.append(jnp.where(tile > k, value, 0.0))
        gpart[0:nb] = dot(z[1], cb[1])
        gpart[nb : 2 * nb] = dot(z[1], cb[0])
        gpart[2 * nb : 3 * nb] = dot(z[0], cb[0])

        def ga_copy(d):
            w = lax.rem(wk + d, T)
            return remote(
                gpart.at[pl.ds(pl.multiple_of(w * piece, 8), piece)],
                grecv.at[wk],
                ga_send.at[d],
                ga_recv.at[wk],
                wrow(w),
                c,
            )

        for d in range(1, T):
            ga_copy(d).start()

        @pl.when(r != 1)
        def _():
            l_copy(1).wait_recv()

        y1 = dot(inv_ref[1].T, z[1])
        y0 = dot(inv_ref[0].T, z[0] - dot(l10[...].T, y1))
        y0, y1 = 0.5 * y0, 0.5 * y1
        ybuf[0] = y0
        ybuf[1] = y1
        ybuf[2] = y0.T
        ybuf[3] = y1.T

        def row_copy(k):
            return remote(
                ybuf.at[k], rowupd.at[wk], y_send.at[k], row_recv.at[wk], k, c
            )

        def col_copy(k):
            return remote(
                ybuf.at[2 + k],
                colupd.at[dst_slot],
                y_send.at[2 + k],
                col_recv.at[dst_slot],
                dst_row,
                k,
            )

        total = gpart[pl.ds(pl.multiple_of(wk * piece, 8), piece)]
        for d in range(1, T):
            other = lax.rem(wk + T - d, T)
            remote(
                gpart.at[pl.ds(0, piece)],
                grecv.at[other],
                ga_send.at[0],
                ga_recv.at[other],
                r,
                c,
            ).wait_recv()
            total = total + grecv[other]
        gred[...] = total

        def gb_copy(k, source):
            return remote(
                gred, g2.at[source], gb_send.at[k], gb_recv.at[source], r, k
            )

        for k in range(2):

            @pl.when(c != k)
            def _():
                gb_copy(k, c).start()

        @pl.when(c < 2)
        def _():
            summed = gred[...]
            for d in range(1, n_col):
                other = lax.rem(c + d, n_col)
                gb_copy(0, other).wait_recv()
                summed = summed + g2[other]
            gsum[...] = summed

            def gc_copy(k):
                return remote(
                    gsum, g3.at[wk], gc_send.at[k], gc_recv.at[wk], k, c
                )

            for k in range(2):

                @pl.when(r != k)
                def _():
                    gc_copy(k).start()

                @pl.when(r == k)
                def _():
                    g3[wk] = gsum[...]

            for k in range(2):

                @pl.when(r != k)
                def _():
                    gc_copy(k).wait_send()

        for k in range(2):
            own_col = (dst_row == r) & (c == k)

            @pl.when(r != k)
            def _():
                row_copy(k).start()

            @pl.when(r == k)
            def _():
                rowupd[wk] = ybuf[k]

            @pl.when(jnp.logical_not(own_col))
            def _():
                col_copy(k).start()

            @pl.when(own_col)
            def _():
                colupd[dst_slot] = ybuf[2 + k]

        for d in range(1, T):
            ga_copy(d).wait_send()
        for k in range(2):

            @pl.when(r != k)
            def _():
                row_copy(k).wait_send()

            @pl.when(jnp.logical_not((dst_row == r) & (c == k)))
            def _():
                col_copy(k).wait_send()

            @pl.when(c != k)
            def _():
                gb_copy(k, c).wait_send()

    @pl.when(jnp.logical_not(is_worker) & (r != 1))
    def _():
        l_copy(1).wait_recv()

    @pl.when(r == 0)
    def _():
        raw_copy().wait_recv()

    @pl.when((r < 2) & (c < 2))
    def _():
        for w in range(T):

            @pl.when(wrow(w) != r)
            def _():
                remote(
                    gsum, g3.at[w], gc_send.at[0], gc_recv.at[w], r, c
                ).wait_recv()

        gram = g3[...].reshape(3 * nb, nb)
        inv0, inv1, off = inv_ref[0], inv_ref[1], l10[...]
        g1 = dot(inv1.T, gram[0:nb])
        p1 = inner_block(raw1[0], raw1[1], g1)
        cross = dot(inv1.T, gram[nb : 2 * nb])
        at = pl.ds(0, nb, stride=T)

        @pl.when((r == 1) & (c == 1))
        def _():
            out_ref[at, :] = out_ref[at, :] + mixed_block(p1, inv1)

        @pl.when(r + c == 1)
        def _():
            moved = dot(inv1, dot(off, inv0))
            base = dot(cross, inv0)
            change = 0.5 * base + 0.5 * dot(inv1.T, dot(p1 + p1.T, moved))

            @pl.when(c == 0)
            def _():
                out_ref[at, :] = out_ref[at, :] - change

            @pl.when(c == 1)
            def _():
                out_ref[at, :] = out_ref[at, :] - change.T

        @pl.when((r == 0) & (c == 0))
        def _():
            moved = dot(inv1, off)
            tied = dot(off.T, cross)
            base = dot(inv0.T, gram[2 * nb : 3 * nb] - tied - tied.T)
            g0 = base - dot(dot(moved, inv0).T, dot(p1 + p1.T, moved))
            p0 = inner_block(raw[0], raw[1], g0)
            out_ref[at, :] = out_ref[at, :] + mixed_block(p0, inv0)

    @pl.when(c < 2)
    def _():
        for i in range(R):
            src_col, src_row = slot_source(i)

            @pl.when(jnp.logical_not((src_col == c) & (src_row == r)))
            def _():
                remote(
                    ybuf.at[0], colupd.at[i], y_send.at[0], col_recv.at[i], r, c
                ).wait_recv()

            at = pl.ds(i * nb * T, nb, stride=T)
            out_ref[at, :] = out_ref[at, :] + colupd[i]

    @pl.when(r < 2)
    def _():
        for t in range(T):

            @pl.when(wrow(t) != r)
            def _():
                remote(
                    ybuf.at[0], rowupd.at[t], y_send.at[0], row_recv.at[t], r, c
                ).wait_recv()

            at = pl.ds(t, nb, stride=T)
            out_ref[at, :] = out_ref[at, :] + rowupd[t]

    for i in range(R):
        src_col, src_row = slot_source(i)

        @pl.when((src_col == c) & (src_row != r))
        def _():
            cb_copy(i, src_row).wait_send()

    @pl.when(r == 1)
    def _():
        raw_copy().wait_send()
        for d in range(1, n_row):
            l_copy(d).wait_send()

    for d in range(half):
        pre_copy(d).wait_send()

        @pl.when(wrow(2 * pair(d) + side) != r)
        def _():
            p_copy(d).wait_send()


def per_device(n_row, n_col, trail_adjoint, factor_panels, factor_adjoint, diag_inverse):
    R, _, nb, T, _, _ = trail_adjoint.shape
    f32 = jnp.float32
    piece = 3 * nb // T
    dma = pltpu.SemaphoreType.DMA
    vmem = pl.BlockSpec(memory_space=pltpu.VMEM)
    out = pl.pallas_call(
        functools.partial(kernel, (n_row, n_col, R, T, nb)),
        out_shape=jax.ShapeDtypeStruct((R * nb * T, nb), f32),
        in_specs=[pl.BlockSpec(memory_space=pltpu.HBM)] * 4,
        out_specs=vmem,
        scratch_shapes=[
            pltpu.VMEM((R * nb * 2, nb), f32),
            pltpu.VMEM((R * nb * 2, nb), f32),
            pltpu.VMEM((2, nb, nb), f32),
            pltpu.VMEM((T // 2, 2 * nb, nb), f32),
            pltpu.VMEM((R, 4, nb, nb), f32),
            pltpu.VMEM((2, nb, nb), f32),
            pltpu.VMEM((2, nb, nb), f32),
            pltpu.VMEM((nb, nb), f32),
            pltpu.VMEM((2, nb, nb), f32),
            pltpu.VMEM((T, 2 * nb, nb), f32),
            pltpu.VMEM((n_row // 2, 2 * nb, nb), f32),
            pltpu.VMEM((3 * nb, nb), f32),
            pltpu.VMEM((T, piece, nb), f32),
            pltpu.VMEM((piece, nb), f32),
            pltpu.VMEM((n_col, piece, nb), f32),
            pltpu.VMEM((piece, nb), f32),
            pltpu.VMEM((T, piece, nb), f32),
            pltpu.VMEM((4, nb, nb), f32),
            pltpu.VMEM((T, nb, nb), f32),
            pltpu.VMEM((R, nb, nb), f32),
            dma((R,)),
            dma,
            dma((n_row,)),
            dma,
            dma((2,)),
            dma((T // 2,)),
            dma((n_row // 2,)),
            dma((T,)),
            dma((T,)),
            dma((2,)),
            dma((n_col,)),
            dma((2,)),
            dma((T,)),
            dma((4,)),
            dma((T,)),
            dma((R,)),
            dma((4,)),
            dma((T // 2,)),
            dma((T // 2,)),
        ],
        compiler_params=pltpu.CompilerParams(
            collective_id=0, has_side_effects=True, vmem_limit_bytes=50 << 20
        ),
    )(
        trail_adjoint.reshape(R * nb * T, nb),
        factor_panels.reshape(R * nb * 2, nb),
        factor_adjoint.reshape(R * nb * 2, nb),
        diag_inverse,
    )
    return out.reshape(trail_adjoint.shape)


def solution(mesh):
    placed = (
        P(None, "row", None, None, "col", None),
        P(None, "row", None, None, None),
        P(None, "row", None, None, None),
        P(),
    )
    return jax.shard_map(
        functools.partial(per_device, mesh.shape["row"], mesh.shape["col"]),
        mesh=mesh,
        in_specs=placed,
        out_specs=P(None, "row", None, None, "col", None),
        check_vma=False,
    )
```
